256 devices in a mesh: seq: 64 (over z, x, core), head: 4 (over y).
Axes of the slice: x: 4, y: 4, z: 8, core: 2. Of those that a mesh axis runs over, the one named last changes fastest.
Arguments:
- query: bfloat16 [24576, 2048], P('seq', 'head'), may hold values from -200 to 200
- key: bfloat16 [24576, 2048], P('seq', 'head'), may hold values from -6 to 6
- value: bfloat16 [24576, 2048], P('seq', 'head'), may hold values from -6 to 6
- mixed_grad: bfloat16 [24576, 4096], P('seq', 'head'), may hold values from -6 to 6
- out_weight: bfloat16 [2048, 4096], P('head', 'seq'), may hold values from -0.125 to 0.125
- cluster: int32 [16, 24576, 1], P('head', 'seq'), may hold values from 0 to 63; in each aligned block of 384 rows (0 to 383, 384 to 767, ..., all dimensions but the last counted through in order) at most 12 rows name the same one
Outputs:
- mixed: bfloat16 [24576, 4096], P('seq', 'head')
- query_grad: bfloat16 [24576, 2048], P('seq', 'head')
- key_grad: bfloat16 [24576, 2048], P('seq', 'head')
- value_grad: bfloat16 [24576, 2048], P('seq', 'head')
The draws below stay inside these ranges and needn't reach their ends.
Inputs may be any that keep to these rules, and one draw needn't show every extreme that they name: In each aligned block of 384 tokens of one head (the tokens of one index of seq) no cluster is named by more than 12 tokens, and some block reaches 12.
All inputs are finite; a program needn't handle non-finite values.
Results may differ from the reference program's by a relative error of at most 0.0058.
Values may be sent and summed in bfloat16 or wider, within the bound.
No kernel may reach another device: no remote copies, remote signals or barrier semaphores. Data moves between devices by JAX's collectives and lax.ppermute only.
A program may use at most 128 MiB of HBM per device.

```python
import math
import jax
import jax.numpy as jnp
import numpy as np
from jax import lax

D = 4096
HEADS = 16
HD = 128
CLUSTERS = 64
TOK_DEV = 384
CAP = 12
TOKENS = 24576
N_SEQ = 64


def shared_keys(key):
    return jax.random.normal(key, (TOKENS, HEADS * HD), jnp.float32)


def draw_key(key, part):
    base = shared_keys(key)
    return jnp.clip(base, -6.0, 6.0).astype(jnp.bfloat16)


def draw_query(key, part):
    key = jax.random.fold_in(key, 7)
    fresh = jax.random.normal(key, (TOKENS, HEADS * HD), jnp.float32)
    return jnp.clip(fresh, -6.0, 6.0).astype(jnp.bfloat16)


def shard_levels(own_key, extent, cuts, least, largest):
    def one(dim, shards_of):
        steps = jax.random.uniform(jax.random.fold_in(jax.random.fold_in(own_key, 6), dim), (shards_of,), jnp.float32, least / len(cuts), largest / len(cuts))
        return jnp.repeat(jnp.exp(steps), extent[dim] // shards_of).reshape((-1,) + (1,) * (len(extent) - dim - 1))

    loudness = one(*cuts[0])
    for cut in cuts[1:]:
        loudness = loudness * one(*cut)
    return loudness


def shared_out(stream_key, own, number, rows, count, top, bound, lean):
    sequence = jax.random.permutation(stream_key, count)
    packed, usual = load_shares(count, rows * top, bound, lean, True), load_shares(count, rows * top, bound, lean, False)
    places = jnp.arange(count)

    def named(sizes, offset_by):
        used = int((sizes > 0).sum())
        fixed = max(1, used // 4)
        shifted = fixed + (places - fixed + offset_by * (used - fixed)) % max(1, count - fixed)
        return jnp.zeros((count,), jnp.int32).at[sequence[jnp.where(places < fixed, places, shifted)]].set(jnp.asarray(sizes, jnp.int32))

    sizes = jnp.where(number % 4 == 0, named(packed, number // 4), named(usual, number - number // 4 - 1))
    mixed = jax.random.permutation(jax.random.fold_in(own, 3), count)
    donor, sink = mixed[0:count // 2 * 2:2], mixed[1:count // 2 * 2:2]
    margin = jnp.minimum(sizes[donor] - 1, bound - sizes[sink]) // 2
    margin = jnp.where((donor == sequence[0]) | (sink == sequence[0]) | (sizes[sink] == 0), 0, jnp.maximum(margin, 0))
    shifted = jax.random.randint(jax.random.fold_in(own, 4), (count // 2,), 0, 1 << 20) % (margin + 1)
    sizes = sizes.at[donor].add(-shifted).at[sink].add(shifted)
    labels = jnp.searchsorted(jnp.cumsum(sizes), jnp.arange(rows * top), side="right").astype(jnp.int32)
    listing = labels.reshape(top, rows).T
    listing = listing[jax.random.permutation(jax.random.fold_in(own, 1), rows)]
    offset_by = jax.random.randint(jax.random.fold_in(own, 2), (rows, 1), 0, top)
    return jnp.take_along_axis(listing, (jnp.arange(top)[None, :] + offset_by) % top, axis=1)


def load_shares(count, total, limit, lean, full):
    loads = [(1 << 20) // math.isqrt(rank ** lean) + 1 for rank in range(1, count + 1)]
    largest = limit if full else min(limit, max(-(-total // count), total * loads[0] // sum(loads)))
    least = 1 if total - largest >= count - 1 else 0
    given, spare = [largest] + [least] * (count - 1), total - largest - least * (count - 1)
    while spare > 0:
        candidates = [i for i in range(1, count) if given[i] < largest] or [i for i in range(1, count) if given[i] < limit]
        mass, remaining = sum([loads[i] for i in candidates]), spare
        for i in candidates:
            more = min(limit - given[i], max(1, remaining * loads[i] // mass), spare)
            given[i] = given[i] + more
            spare = spare - more
    return np.array(given)


def noise(stream_key, extent, width, limit, cuts=(), kind=jnp.bfloat16):
    array = width * jax.random.normal(stream_key, extent, jnp.float32)
    if cuts:
        array = array * shard_levels(stream_key, extent, cuts, -0.22, 0.18)
    return jnp.clip(array, -limit, limit).astype(kind)


def setup_inputs(seed: int = 0) -> dict:
    streams_of = jax.random.split(jax.random.key(seed), 7)
    query = draw_query(jax.random.fold_in(streams_of[6], 71), 0)
    key = draw_key(jax.random.fold_in(streams_of[6], 71), 0)
    value = noise(streams_of[2], (TOKENS, HEADS * HD), 1.0, 6.0, ((0, 64), (1, 4)))
    mixed_grad = noise(streams_of[3], (TOKENS, D), 1.0, 6.0, ((0, 64), (1, 4)))
    out_weight = noise(streams_of[4], (HEADS * HD, D), (HEADS * HD) ** -0.5, 0.125, ((0, 4), (1, 64)))
    cluster_keys = jax.random.split(jax.random.fold_in(streams_of[5], 1), HEADS * TOKENS // TOK_DEV)
    cluster_turns = jax.random.permutation(jax.random.fold_in(streams_of[5], 3), HEADS * TOKENS // TOK_DEV)
    cluster = jax.vmap(lambda own, number: shared_out(jax.random.fold_in(streams_of[5], 2), own, number, TOK_DEV, CLUSTERS, 1, CAP, 1))(cluster_keys, cluster_turns).reshape((HEADS, TOKENS, 1))
    return dict(query=query, key=key, value=value, mixed_grad=mixed_grad, out_weight=out_weight, cluster=cluster)


def attend(q, k, v, g, same):
    scale = 1.0 / math.sqrt(q.shape[-1])
    scores = jnp.dot(q, k.T, preferred_element_type=jnp.float32) * scale
    scores = jnp.where(same, scores, -1e+30)
    top = lax.optimization_barrier(jnp.max(scores, axis=-1, keepdims=True))
    weights = jnp.where(same, jnp.exp(scores - top), 0.0)
    probs = weights / lax.optimization_barrier(jnp.sum(weights, axis=-1, keepdims=True))
    probs16 = probs.astype(jnp.bfloat16)
    attended = jnp.dot(probs16, v, preferred_element_type=jnp.float32).astype(jnp.bfloat16)
    dprobs = jnp.dot(g, v.T, preferred_element_type=jnp.float32)
    delta = lax.optimization_barrier(jnp.sum(probs * dprobs, axis=-1, keepdims=True))
    dscores = (probs * (dprobs - delta)).astype(jnp.bfloat16)
    query_grad = (jnp.dot(dscores, k, preferred_element_type=jnp.float32) * scale).astype(jnp.bfloat16)
    key_grad = (jnp.dot(dscores.T, q, preferred_element_type=jnp.float32) * scale).astype(jnp.bfloat16)
    value_grad = jnp.dot(probs16.T, g, preferred_element_type=jnp.float32).astype(jnp.bfloat16)
    return (attended, query_grad, key_grad, value_grad)

def one_head(qh, kh, vh, gh, ids):
    members = CAP * N_SEQ
    order = jnp.argsort(ids, stable=True).astype(jnp.int32)
    counts = lax.optimization_barrier(jnp.sum((ids[:, None] == jnp.arange(CLUSTERS, dtype=jnp.int32)[None, :]).astype(jnp.int32), axis=0))
    starts = (jnp.cumsum(counts) - counts).astype(jnp.int32)
    padded_order = jnp.concatenate([order, jnp.full((members,), TOKENS, jnp.int32)])
    eye = jnp.eye(members, dtype=bool)

    def per_cluster(c):
        idx = lax.dynamic_slice(padded_order, (starts[c].astype(jnp.int32),), (members,))
        valid = jnp.arange(members, dtype=jnp.int32) < counts[c]
        safe = jnp.where(valid, idx, 0)
        same = valid[None, :] | eye
        rows_live = valid[:, None]
        q_rows = jnp.where(rows_live, qh[safe], jnp.zeros((), qh.dtype))
        k_rows = jnp.where(rows_live, kh[safe], jnp.zeros((), kh.dtype))
        v_rows = jnp.where(rows_live, vh[safe], jnp.zeros((), vh.dtype))
        g_rows = jnp.where(rows_live, gh[safe], jnp.zeros((), gh.dtype))
        results = attend(q_rows, k_rows, v_rows, g_rows, same)
        return (results, jnp.where(valid, idx, TOKENS))
    results, where_to = lax.map(per_cluster, jnp.arange(CLUSTERS, dtype=jnp.int32))
    flat_to = where_to.reshape(-1)
    outs = []
    for part in results:
        placed = jnp.zeros((TOKENS, qh.shape[1]), jnp.bfloat16)
        outs.append(placed.at[flat_to].set(part.reshape(-1, qh.shape[1]), mode='drop'))
    return outs

def reference(query, key, value, mixed_grad, out_weight, cluster):
    grad_att = jnp.dot(mixed_grad, out_weight.T, preferred_element_type=jnp.float32).astype(jnp.bfloat16)
    columns = [[], [], [], []]
    for head in range(HEADS):
        lo = head * HD
        outs = one_head(query[:, lo:lo + HD], key[:, lo:lo + HD], value[:, lo:lo + HD], grad_att[:, lo:lo + HD], cluster[head, :, 0])
        for slot_list, part in zip(columns, outs):
            slot_list.append(part)
    attended, query_grad, key_grad, value_grad = [jnp.concatenate(c, axis=1) for c in columns]
    mixed = jnp.dot(attended, out_weight, preferred_element_type=jnp.float32).astype(jnp.bfloat16)
    return (mixed, query_grad, key_grad, value_grad)
```

```python
import functools
import math

import jax
import jax.numpy as jnp
from jax import lax
from jax.experimental import pallas as pl
from jax.experimental.pallas import tpu as pltpu
from jax.sharding import PartitionSpec as P

HD = 128
CLUSTERS = 64
CAP = 12
EMPTY_MARK = 128.0
SCALE = 1.0 / math.sqrt(HD)
LOG2E = math.log2(math.e)

VMEM = pl.BlockSpec(memory_space=pltpu.VMEM)
SMEM = pl.BlockSpec(memory_space=pltpu.SMEM)
PARAMS = pltpu.CompilerParams(vmem_limit_bytes=56 * 1024 * 1024)


def dot_nt(a, b):
    return lax.dot_general(a, b, (((1,), (1,)), ((), ())), preferred_element_type=jnp.float32)


def dot_tn(a, b):
    return lax.dot_general(a, b, (((0,), (0,)), ((), ())), preferred_element_type=jnp.float32)


def dot_nn(a, b):
    return jnp.dot(a, b, preferred_element_type=jnp.float32)


def head_cols(h):
    return pl.ds(h * HD, HD)


def slot_onehot(slot_row):
    tokens = slot_row.shape[1]
    place = lax.broadcasted_iota(jnp.int32, (CLUSTERS * CAP, tokens), 0)
    return jnp.where(place == slot_row, 1.0, 0.0).astype(jnp.bfloat16)


def token_onehot(slot_row):
    tokens = slot_row.shape[1]
    spread = jnp.broadcast_to(slot_row.astype(jnp.float32), (HD, tokens)).T
    lane = lax.broadcasted_iota(jnp.int32, (tokens, HD), 1).astype(jnp.float32)
    pieces = [
        jnp.where(spread == lane + float(start), 1.0, 0.0).astype(jnp.bfloat16)
        for start in range(0, CLUSTERS * CAP, HD)
    ]
    return jnp.concatenate(pieces, axis=1)


def pack_kernel(ids_ref, q_ref, k_ref, v_ref, out_ref, slots_ref, wide):
    heads, tokens = ids_ref.shape
    rows = CLUSTERS * CAP
    before = (
        lax.broadcasted_iota(jnp.int32, (tokens, tokens), 0)
        < lax.broadcasted_iota(jnp.int32, (tokens, tokens), 1)
    )
    before = jnp.where(before, 1.0, 0.0).astype(jnp.bfloat16)
    cluster = lax.broadcasted_iota(jnp.int32, (CLUSTERS, tokens), 0)
    ones = jnp.ones((tokens, HD), jnp.bfloat16)
    first_lane = lax.broadcasted_iota(jnp.int32, (rows, HD), 1) == 0
    for h in range(heads):
        ids = ids_ref[h : h + 1, :]
        named = jnp.where(cluster == ids, 1.0, 0.0)
        earlier = dot_nn(named.astype(jnp.bfloat16), before)
        rank = jnp.sum(named * earlier, axis=0, keepdims=True)
        slot = ids * CAP + rank.astype(jnp.int32)
        slots_ref[h : h + 1, :] = slot
        data = jnp.concatenate(
            [q_ref[:, head_cols(h)], k_ref[:, head_cols(h)], v_ref[:, head_cols(h)], ones], axis=1
        )
        placed = dot_nn(slot_onehot(slot), data)
        used = placed[:, 3 * HD :]
        mark = jnp.where(first_lane, (1.0 - used) * EMPTY_MARK, 0.0)
        where = pl.ds(h, rows, stride=heads)
        wide[0, where, :] = placed[:, :HD]
        wide[1, where, :] = placed[:, HD : 2 * HD] + mark
        wide[2, where, :] = placed[:, 2 * HD : 3 * HD]
    for t in range(3):
        out_ref[:, t * HD : (t + 1) * HD] = wide[t].astype(jnp.bfloat16)


def grad_kernel(y_ref, slots_ref, m0, m1, m2, m3, wt_ref, out_ref, wide):
    heads = slots_ref.shape[0]
    rows = CLUSTERS * CAP
    y = y_ref[0]
    total = None
    for d, m_ref in enumerate((m0, m1, m2, m3)):
        cols = m_ref.shape[1]
        start = pl.multiple_of(lax.rem(y + (4 - d), 4) * cols, cols)
        part = dot_nn(m_ref[...], wt_ref[pl.ds(start, cols), :])
        total = part if total is None else total + part
    grad = total.astype(jnp.bfloat16)
    for h in range(heads):
        placed = dot_nn(slot_onehot(slots_ref[h : h + 1, :]), grad[:, h * HD : (h + 1) * HD])
        wide[pl.ds(h, rows, stride=heads), :] = placed
    out_ref[...] = wide[...].astype(jnp.bfloat16)


def forward_kernel(x_ref, att_ref, heads_ref, probs_ref, wide, back):
    heads = pl.num_programs(0)
    rows = CLUSTERS * CAP
    h = pl.program_id(0)

    @pl.when(h == 0)
    def _():
        for t in range(3):
            wide[t] = x_ref[:, t * HD : (t + 1) * HD].astype(jnp.float32)

    where = pl.ds(h, rows, stride=4)
    q = wide[0, where, :].astype(jnp.bfloat16)
    k_wide = wide[1, where, :]
    k = k_wide.astype(jnp.bfloat16)
    v = wide[2, where, :].astype(jnp.bfloat16)
    heads_ref[0] = q
    heads_ref[1] = k
    heads_ref[2] = v
    bias = jnp.where(k_wide[:, :1] > EMPTY_MARK / 2, -1e30, 0.0)
    scores = dot_nt(k, q) + bias
    top = jnp.max(scores, axis=0, keepdims=True)
    weights = jnp.exp2((scores - top) * (SCALE * LOG2E))
    probs = weights * (1.0 / jnp.sum(weights, axis=0, keepdims=True))
    probs_ref[0] = probs
    back[where, :] = dot_tn(v, probs.astype(jnp.bfloat16)).T

    @pl.when(h == heads - 1)
    def _():
        att_ref[...] = back[...].astype(jnp.bfloat16)


def backward_kernel(g_ref, heads_ref, probs_ref, out_ref, wide, back):
    heads = pl.num_programs(0)
    rows = CLUSTERS * CAP
    h = pl.program_id(0)

    @pl.when(h == 0)
    def _():
        wide[...] = g_ref[...].astype(jnp.float32)

    where = pl.ds(h, rows, stride=4)
    g = wide[where, :].astype(jnp.bfloat16)
    q, k, v = heads_ref[0], heads_ref[1], heads_ref[2]
    probs = probs_ref[0]
    dprobs = dot_nt(v, g)
    delta = jnp.sum(probs * dprobs, axis=0, keepdims=True)
    dscores = (probs * (dprobs - delta)).astype(jnp.bfloat16)
    back[0, where, :] = dot_tn(k, dscores).T * SCALE
    back[1, where, :] = dot_nn(dscores, q) * SCALE
    back[2, where, :] = dot_nn(probs.astype(jnp.bfloat16), g)

    @pl.when(h == heads - 1)
    def _():
        for t in range(3):
            out_ref[:, t * HD : (t + 1) * HD] = back[t].astype(jnp.bfloat16)


def mixed_kernel(y_ref, slots_ref, att_ref, wt_ref, own_ref, s1, s2, s3, wide):
    heads = slots_ref.shape[0]
    rows = CLUSTERS * CAP
    y = y_ref[0]
    wide[...] = att_ref[...].astype(jnp.float32)
    pieces = []
    for h in range(heads):
        held = wide[pl.ds(h, rows, stride=heads), :].astype(jnp.bfloat16)
        pieces.append(dot_nn(token_onehot(slots_ref[h : h + 1, :]), held).astype(jnp.bfloat16))
    att = jnp.concatenate(pieces, axis=1)
    for d, s_ref in enumerate((own_ref, s1, s2, s3)):
        cols = s_ref.shape[1]
        start = pl.multiple_of(lax.rem(y + d, 4) * cols, cols)
        s_ref[...] = dot_nt(att, wt_ref[pl.ds(start, cols), :]).astype(s_ref.dtype)


def unpack_kernel(slots_ref, x_ref, dq_ref, dk_ref, dv_ref, wide):
    heads = slots_ref.shape[0]
    rows = CLUSTERS * CAP
    for t in range(3):
        wide[t] = x_ref[:, t * HD : (t + 1) * HD].astype(jnp.float32)
    for h in range(heads):
        where = pl.ds(h, rows, stride=heads)
        held = jnp.concatenate(
            [wide[t, where, :].astype(jnp.bfloat16) for t in range(3)], axis=1
        )
        got = dot_nn(token_onehot(slots_ref[h : h + 1, :]), held).astype(jnp.bfloat16)
        for t, ref in enumerate((dq_ref, dk_ref, dv_ref)):
            ref[:, head_cols(h)] = got[:, t * HD : (t + 1) * HD]


def call(kernel, out, scratch, count, smem_first=False):
    specs = [VMEM] * count
    if smem_first:
        specs[0] = SMEM
    return pl.pallas_call(
        kernel,
        out_shape=out,
        in_specs=specs,
        out_specs=jax.tree.map(lambda _: VMEM, out),
        scratch_shapes=scratch,
        compiler_params=PARAMS,
    )


def sds(shape, dtype=jnp.bfloat16):
    return jax.ShapeDtypeStruct(shape, dtype)


def exchange(x):
    return lax.all_to_all(x, "seq", split_axis=0, concat_axis=0, tiled=True)


def local(query, key, value, mixed_grad, out_weight, cluster):
    tokens = query.shape[0]
    heads = cluster.shape[0]
    rows = CLUSTERS * CAP
    slots_all = heads * rows
    y = lax.axis_index("head").astype(jnp.int32).reshape(1)

    def turn(x, d):
        return lax.ppermute(x, "head", [(i, (i + d) % 4) for i in range(4)])

    wt = lax.all_gather(out_weight.T, "seq", axis=0, tiled=True)
    grads = [mixed_grad] + [turn(mixed_grad, d) for d in (1, 2, 3)]

    payload, slots = call(
        pack_kernel,
        (sds((slots_all, 3 * HD)), sds((heads, tokens), jnp.int32)),
        [pltpu.VMEM((3, slots_all, HD), jnp.float32)],
        4,
    )(cluster.reshape(heads, tokens), query, key, value)
    arrived = exchange(payload)

    att, held, probs = pl.pallas_call(
        forward_kernel,
        grid=(heads,),
        out_shape=(
            sds((slots_all, HD)),
            sds((heads * 3, rows, HD)),
            sds((heads, rows, rows), jnp.float32),
        ),
        in_specs=[pl.BlockSpec((slots_all, 3 * HD), lambda h: (0, 0))],
        out_specs=(
            pl.BlockSpec((slots_all, HD), lambda h: (0, 0)),
            pl.BlockSpec((3, rows, HD), lambda h: (h, 0, 0)),
            pl.BlockSpec((1, rows, rows), lambda h: (h, 0, 0)),
        ),
        scratch_shapes=[
            pltpu.VMEM((3, slots_all, HD), jnp.float32),
            pltpu.VMEM((slots_all, HD), jnp.float32),
        ],
        compiler_params=PARAMS,
    )(arrived)

    grad_payload = call(
        grad_kernel,
        sds((slots_all, HD)),
        [pltpu.VMEM((slots_all, HD), jnp.float32)],
        7,
        smem_first=True,
    )(y, slots, *grads, wt)
    att_back = exchange(att)
    grad_arrived = exchange(grad_payload)

    done = pl.pallas_call(
        backward_kernel,
        grid=(heads,),
        out_shape=sds((slots_all, 3 * HD)),
        in_specs=[
            pl.BlockSpec((slots_all, HD), lambda h: (0, 0)),
            pl.BlockSpec((3, rows, HD), lambda h: (h, 0, 0)),
            pl.BlockSpec((1, rows, rows), lambda h: (h, 0, 0)),
        ],
        out_specs=pl.BlockSpec((slots_all, 3 * HD), lambda h: (0, 0)),
        scratch_shapes=[
            pltpu.VMEM((slots_all, HD), jnp.float32),
            pltpu.VMEM((3, slots_all, HD), jnp.float32),
        ],
        compiler_params=PARAMS,
    )(grad_arrived, held, probs)
    back = exchange(done)

    cols = mixed_grad.shape[1]
    own, *sends = call(
        mixed_kernel,
        (sds((tokens, cols), jnp.float32),) + (sds((tokens, cols)),) * 3,
        [pltpu.VMEM((slots_all, HD), jnp.float32)],
        4,
        smem_first=True,
    )(y, slots, att_back, wt)
    mixed = own
    for d, part in zip((1, 2, 3), sends):
        mixed = mixed + turn(part, d).astype(jnp.float32)
    mixed = mixed.astype(jnp.bfloat16)

    query_grad, key_grad, value_grad = call(
        unpack_kernel,
        (sds((tokens, heads * HD)),) * 3,
        [pltpu.VMEM((3, slots_all, HD), jnp.float32)],
        2,
    )(slots, back)
    return (mixed, query_grad, key_grad, value_grad)


def solution(mesh):
    placed = (
        P("seq", "head"),
        P("seq", "head"),
        P("seq", "head"),
        P("seq", "head"),
        P("head", "seq"),
        P("head", "seq", None),
    )
    return jax.shard_map(
        local,
        mesh=mesh,
        in_specs=placed,
        out_specs=(P("seq", "head"), P("seq", "head"), P("seq", "head"), P("seq", "head")),
        check_vma=False,
    )
```

```python
import functools
import math

import jax
import jax.numpy as jnp
from jax import lax
from jax.experimental import pallas as pl
from jax.experimental.pallas import tpu as pltpu
from jax.sharding import PartitionSpec as P

HD = 128
CLUSTERS = 64
CAP = 12
EMPTY_MARK = 128.0
SCALE = 1.0 / math.sqrt(HD)
LOG2E = math.log2(math.e)

VMEM = pl.BlockSpec(memory_space=pltpu.VMEM)
PARAMS = pltpu.CompilerParams(vmem_limit_bytes=56 * 1024 * 1024)


def dot_nt(a, b):
    return lax.dot_general(a, b, (((1,), (1,)), ((), ())), preferred_element_type=jnp.float32)


def dot_tn(a, b):
    return lax.dot_general(a, b, (((0,), (0,)), ((), ())), preferred_element_type=jnp.float32)


def dot_nn(a, b):
    return jnp.dot(a, b, preferred_element_type=jnp.float32)


def head_cols(h):
    return pl.ds(h * HD, HD)


def slot_onehot(slot_row):
    tokens = slot_row.shape[1]
    place = lax.broadcasted_iota(jnp.int32, (CLUSTERS * CAP, tokens), 0)
    return jnp.where(place == slot_row, 1.0, 0.0).astype(jnp.bfloat16)


def token_onehot(slot_row):
    tokens = slot_row.shape[1]
    spread = jnp.broadcast_to(slot_row.astype(jnp.float32), (HD, tokens)).T
    lane = lax.broadcasted_iota(jnp.int32, (tokens, HD), 1).astype(jnp.float32)
    pieces = [
        jnp.where(spread == lane + float(start), 1.0, 0.0).astype(jnp.bfloat16)
        for start in range(0, CLUSTERS * CAP, HD)
    ]
    return jnp.concatenate(pieces, axis=1)


def pack_kernel(ids_ref, q_ref, k_ref, v_ref, out_ref, slots_ref, wide):
    heads, _, tokens = ids_ref.shape
    rows = CLUSTERS * CAP
    before = (
        lax.broadcasted_iota(jnp.int32, (tokens, tokens), 0)
        < lax.broadcasted_iota(jnp.int32, (tokens, tokens), 1)
    )
    before = jnp.where(before, 1.0, 0.0).astype(jnp.bfloat16)
    cluster = lax.broadcasted_iota(jnp.int32, (CLUSTERS, tokens), 0)
    ones = jnp.ones((tokens, HD), jnp.bfloat16)
    first_lane = lax.broadcasted_iota(jnp.int32, (rows, HD), 1) == 0
    for h in range(heads):
        ids = ids_ref[h]
        named = jnp.where(cluster == ids, 1.0, 0.0)
        earlier = dot_nn(named.astype(jnp.bfloat16), before)
        rank = jnp.sum(named * earlier, axis=0, keepdims=True)
        slot = ids * CAP + rank.astype(jnp.int32)
        slots_ref[h : h + 1, :] = slot
        data = jnp.concatenate(
            [q_ref[:, head_cols(h)], k_ref[:, head_cols(h)], v_ref[:, head_cols(h)], ones], axis=1
        )
        placed = dot_nn(slot_onehot(slot), data)
        used = placed[:, 3 * HD :]
        mark = jnp.where(first_lane, (1.0 - used) * EMPTY_MARK, 0.0)
        where = pl.ds(h, rows, stride=heads)
        wide[0, where, :] = placed[:, :HD]
        wide[1, where, :] = placed[:, HD : 2 * HD] + mark
        wide[2, where, :] = placed[:, 2 * HD : 3 * HD]
    for t in range(3):
        out_ref[:, t * HD : (t + 1) * HD] = wide[t].astype(jnp.bfloat16)


def grad_kernel(slots_ref, *refs):
    grads, own_core, other_core = refs[:4], refs[4:8], refs[8:12]
    out_ref, wt_ref, wide = refs[12:]
    heads = slots_ref.shape[0]
    rows = CLUSTERS * CAP
    seq, y = lax.axis_index("seq"), lax.axis_index("head")
    x, core = lax.rem(seq // 2, 4), lax.rem(seq, 2)
    depth = own_core[0].shape[0] // 8
    for d in range(4):
        for c, refs_of in enumerate((own_core, other_core)):
            part = lax.rem(x + (4 - d), 4) * 2 + (core if c == 0 else 1 - core)
            for z in range(8):
                start = pl.multiple_of((part + z * 8) * depth, depth)
                wt_ref[pl.ds(start, depth), :] = refs_of[d][z * depth : (z + 1) * depth, :]
    total = None
    for d, m_ref in enumerate(grads):
        cols = m_ref.shape[1]
        start = pl.multiple_of(lax.rem(y + (4 - d), 4) * cols, cols)
        part = dot_nn(m_ref[...], wt_ref[pl.ds(start, cols), :])
        total = part if total is None else total + part
    grad = total.astype(jnp.bfloat16)
    for h in range(heads):
        placed = dot_nn(slot_onehot(slots_ref[h : h + 1, :]), grad[:, h * HD : (h + 1) * HD])
        wide[pl.ds(h, rows, stride=heads), :] = placed
    out_ref[...] = wide[...].astype(jnp.bfloat16)


def split_heads(x_ref, wide):
    for t in range(wide.shape[0]):
        wide[t] = x_ref[:, t * HD : (t + 1) * HD].astype(jnp.float32)


def scores_of(q, k, k_wide):
    first = lax.broadcasted_iota(jnp.int32, k.shape, 1) == 0
    mask = jnp.where(first & (k_wide > EMPTY_MARK / 2), -1e30, 0.0).astype(jnp.bfloat16)
    ones = jnp.ones(q.shape, jnp.bfloat16)
    return dot_nt(jnp.concatenate([k, mask], axis=1), jnp.concatenate([q, ones], axis=1))


def forward_kernel(x_ref, att_ref, heads_ref, probs_ref, att_wide_ref, wide, back):
    rows = CLUSTERS * CAP
    h = pl.program_id(0)

    @pl.when(h == 0)
    def _():
        split_heads(x_ref, wide)

    where = pl.ds(h, rows, stride=x_ref.shape[0] // rows)
    q = wide[0, where, :].astype(jnp.bfloat16)
    k_wide = wide[1, where, :]
    k = k_wide.astype(jnp.bfloat16)
    v = wide[2, where, :].astype(jnp.bfloat16)
    heads_ref[0] = q
    heads_ref[1] = k
    heads_ref[2] = v
    scores = scores_of(q, k, k_wide)
    top = jnp.max(scores, axis=0, keepdims=True)
    weights = jnp.exp2((scores - top) * (SCALE * LOG2E))
    probs = (weights * (1.0 / jnp.sum(weights, axis=0, keepdims=True))).astype(jnp.bfloat16)
    probs_ref[0] = probs
    att = dot_tn(v, probs)
    att_wide_ref[0] = att
    back[where, :] = att.T

    @pl.when(h == pl.num_programs(0) - 1)
    def _():
        att_ref[...] = back[...].astype(jnp.bfloat16)


def backward_kernel(g_ref, heads_ref, probs_ref, att_ref, out_ref, wide, back):
    rows = CLUSTERS * CAP
    h = pl.program_id(0)

    @pl.when(h == 0)
    def _():
        split_heads(g_ref, wide)

    where = pl.ds(h, rows, stride=g_ref.shape[0] // rows)
    g_wide = wide[0, where, :]
    g = g_wide.astype(jnp.bfloat16)
    q, k, v = heads_ref[0], heads_ref[1], heads_ref[2]
    probs = probs_ref[0]
    delta = jnp.sum(g_wide.T * att_ref[0], axis=0, keepdims=True)
    dscores = (probs.astype(jnp.float32) * (dot_nt(v, g) - delta)).astype(jnp.bfloat16)
    back[0, where, :] = dot_tn(k, dscores).T * SCALE
    back[1, where, :] = dot_nn(dscores, q) * SCALE
    back[2, where, :] = dot_nn(probs, g)

    @pl.when(h == pl.num_programs(0) - 1)
    def _():
        for t in range(3):
            out_ref[:, t * HD : (t + 1) * HD] = back[t].astype(jnp.bfloat16)


def mixed_kernel(slots_ref, att_ref, wt_ref, own_ref, s1, s2, s3, wide):
    heads = slots_ref.shape[0]
    rows = CLUSTERS * CAP
    y = lax.axis_index("head")
    wide[...] = att_ref[...].astype(jnp.float32)
    pieces = []
    for h in range(heads):
        held = wide[pl.ds(h, rows, stride=heads), :].astype(jnp.bfloat16)
        pieces.append(dot_nn(token_onehot(slots_ref[h : h + 1, :]), held).astype(jnp.bfloat16))
    att = jnp.concatenate(pieces, axis=1)
    for d, s_ref in enumerate((own_ref, s1, s2, s3)):
        cols = s_ref.shape[1]
        start = pl.multiple_of(lax.rem(y + d, 4) * cols, cols)
        s_ref[...] = dot_nt(att, wt_ref[pl.ds(start, cols), :]).astype(s_ref.dtype)


def unpack_kernel(slots_ref, x_ref, dq_ref, dk_ref, dv_ref, wide):
    heads = slots_ref.shape[0]
    rows = CLUSTERS * CAP
    for t in range(3):
        wide[t] = x_ref[:, t * HD : (t + 1) * HD].astype(jnp.float32)
    for h in range(heads):
        where = pl.ds(h, rows, stride=heads)
        held = jnp.concatenate(
            [wide[t, where, :].astype(jnp.bfloat16) for t in range(3)], axis=1
        )
        got = dot_nn(token_onehot(slots_ref[h : h + 1, :]), held).astype(jnp.bfloat16)
        for t, ref in enumerate((dq_ref, dk_ref, dv_ref)):
            ref[:, head_cols(h)] = got[:, t * HD : (t + 1) * HD]


def call(kernel, out, scratch, count):
    return pl.pallas_call(
        kernel,
        out_shape=out,
        in_specs=[VMEM] * count,
        out_specs=jax.tree.map(lambda _: VMEM, out),
        scratch_shapes=scratch,
        compiler_params=PARAMS,
    )


def sds(shape, dtype=jnp.bfloat16):
    return jax.ShapeDtypeStruct(shape, dtype)


def exchange(x):
    return lax.all_to_all(x, "seq", split_axis=0, concat_axis=0, tiled=True)


def local(query, key, value, mixed_grad, out_weight, cluster):
    tokens = query.shape[0]
    heads = cluster.shape[0]
    rows = CLUSTERS * CAP
    slots_all = heads * rows

    def turn(x, d):
        return lax.ppermute(x, "head", [(i, (i + d) % 4) for i in range(4)])

    spots = [(z, x, c) for z in range(8) for x in range(4) for c in range(2)]

    def place(z, x, c):
        return z % 8 * 8 + x % 4 * 2 + c % 2

    def along(x, move):
        return lax.ppermute(x, "seq", [(place(*s), place(*move(*s))) for s in spots])

    columns = [[place(z, x, c) for z in range(8)] for x in range(4) for c in range(2)]

    shard = out_weight.T
    depth, width = shard.shape
    column = lax.all_to_all(
        jnp.broadcast_to(shard[None], (8, depth, width)).reshape(8 * depth, width),
        "seq",
        split_axis=0,
        concat_axis=0,
        axis_index_groups=columns,
        tiled=True,
    )
    right, left = turn(mixed_grad, 1), turn(mixed_grad, 3)

    payload, slots = call(
        pack_kernel,
        (sds((slots_all, 3 * HD)), sds((heads, tokens), jnp.int32)),
        [pltpu.VMEM((3, slots_all, HD), jnp.float32)],
        4,
    )(cluster.transpose(0, 2, 1), query, key, value)
    payload, column = lax.optimization_barrier((payload, column))
    arrived = exchange(payload)
    own_core = [column] + [along(column, lambda z, x, c, d=d: (z, x + d, c)) for d in (1, 2, 3)]
    other_core = [along(part, lambda z, x, c: (z, x, c + 1)) for part in own_core]
    across = turn(mixed_grad, 2)


    by_head = lambda *shape: pl.BlockSpec(shape, lambda h: (h, 0, 0))
    att, held, probs, att_wide = pl.pallas_call(
        forward_kernel,
        grid=(heads,),
        out_shape=(
            sds((slots_all, HD)),
            sds((heads * 3, rows, HD)),
            sds((heads, rows, rows)),
            sds((heads, HD, rows), jnp.float32),
        ),
        in_specs=[pl.BlockSpec((slots_all, 3 * HD), lambda h: (0, 0))],
        out_specs=(
            pl.BlockSpec((slots_all, HD), lambda h: (0, 0)),
            by_head(3, rows, HD),
            by_head(1, rows, rows),
            by_head(1, HD, rows),
        ),
        scratch_shapes=[
            pltpu.VMEM((3, slots_all, HD), jnp.float32),
            pltpu.VMEM((slots_all, HD), jnp.float32),
        ],
        compiler_params=PARAMS,
    )(arrived)

    grad_payload, wt = call(
        grad_kernel,
        (sds((slots_all, HD)), sds((64 * depth, width))),
        [pltpu.VMEM((slots_all, HD), jnp.float32)],
        13,
    )(slots, mixed_grad, right, across, left, *own_core, *other_core)
    grad_arrived = exchange(grad_payload)
    att, grad_arrived = lax.optimization_barrier((att, grad_arrived))
    att_back = exchange(att)

    done = pl.pallas_call(
        backward_kernel,
        grid=(heads,),
        out_shape=sds((slots_all, 3 * HD)),
        in_specs=[
            pl.BlockSpec((slots_all, HD), lambda h: (0, 0)),
            by_head(3, rows, HD),
            by_head(1, rows, rows),
            by_head(1, HD, rows),
        ],
        out_specs=pl.BlockSpec((slots_all, 3 * HD), lambda h: (0, 0)),
        scratch_shapes=[
            pltpu.VMEM((1, slots_all, HD), jnp.float32),
            pltpu.VMEM((3, slots_all, HD), jnp.float32),
        ],
        compiler_params=PARAMS,
    )(grad_arrived, held, probs, att_wide)
    back = exchange(done)

    cols = mixed_grad.shape[1]
    own, *sends = call(
        mixed_kernel,
        (sds((tokens, cols), jnp.float32),) + (sds((tokens, cols)),) * 3,
        [pltpu.VMEM((slots_all, HD), jnp.float32)],
        3,
    )(slots, att_back, wt)
    mixed = own
    for d, part in zip((1, 2, 3), sends):
        mixed = mixed + turn(part, d).astype(jnp.float32)
    mixed = mixed.astype(jnp.bfloat16)

    query_grad, key_grad, value_grad = call(
        unpack_kernel,
        (sds((tokens, heads * HD)),) * 3,
        [pltpu.VMEM((3, slots_all, HD), jnp.float32)],
        2,
    )(slots, back)
    return (mixed, query_grad, key_grad, value_grad)


def solution(mesh):
    placed = (
        P("seq", "head"),
        P("seq", "head"),
        P("seq", "head"),
        P("seq", "head"),
        P("head", "seq"),
        P("head", "seq", None),
    )
    return jax.shard_map(
        local,
        mesh=mesh,
        in_specs=placed,
        out_specs=(P("seq", "head"), P("seq", "head"), P("seq", "head"), P("seq", "head")),
        check_vma=False,
    )
```

```python
import functools
import math

import jax
import jax.numpy as jnp
from jax import lax
from jax.experimental import pallas as pl
from jax.experimental.pallas import tpu as pltpu
from jax.sharding import PartitionSpec as P

HD = 128
CLUSTERS = 64
CAP = 12
EMPTY_MARK = 128.0
SCALE = 1.0 / math.sqrt(HD)
LOG2E = math.log2(math.e)

VMEM = pl.BlockSpec(memory_space=pltpu.VMEM)
PARAMS = pltpu.CompilerParams(vmem_limit_bytes=32 * 1024 * 1024)


def dot_nt(a, b):
    return lax.dot_general(a, b, (((1,), (1,)), ((), ())), preferred_element_type=jnp.float32)


def dot_tn(a, b):
    return lax.dot_general(a, b, (((0,), (0,)), ((), ())), preferred_element_type=jnp.float32)


def dot_nn(a, b):
    return jnp.dot(a, b, preferred_element_type=jnp.float32)


def head_cols(h):
    return pl.ds(h * HD, HD)


def slot_onehot(slot_row):
    tokens = slot_row.shape[1]
    place = lax.broadcasted_iota(jnp.int32, (CLUSTERS * CAP, tokens), 0)
    return jnp.where(place == slot_row, 1.0, 0.0).astype(jnp.bfloat16)


def token_onehot(slot_row):
    tokens = slot_row.shape[1]
    spread = jnp.broadcast_to(slot_row.astype(jnp.float32), (HD, tokens)).T
    lane = lax.broadcasted_iota(jnp.int32, (tokens, HD), 1).astype(jnp.float32)
    pieces = [
        jnp.where(spread == lane + float(start), 1.0, 0.0).astype(jnp.bfloat16)
        for start in range(0, CLUSTERS * CAP, HD)
    ]
    return jnp.concatenate(pieces, axis=1)


def pack_kernel(ids_ref, q_ref, k_ref, v_ref, out_ref, slots_ref, wide):
    heads, _, tokens = ids_ref.shape
    rows = CLUSTERS * CAP
    before = (
        lax.broadcasted_iota(jnp.int32, (tokens, tokens), 0)
        < lax.broadcasted_iota(jnp.int32, (tokens, tokens), 1)
    )
    before = jnp.where(before, 1.0, 0.0).astype(jnp.bfloat16)
    cluster = lax.broadcasted_iota(jnp.int32, (CLUSTERS, tokens), 0)
    ones = jnp.ones((tokens, HD), jnp.bfloat16)
    first_lane = lax.broadcasted_iota(jnp.int32, (rows, HD), 1) == 0
    for h in range(heads):
        ids = ids_ref[h]
        named = jnp.where(cluster == ids, 1.0, 0.0)
        earlier = dot_nn(named.astype(jnp.bfloat16), before)
        rank = jnp.sum(named * earlier, axis=0, keepdims=True)
        slot = ids * CAP + rank.astype(jnp.int32)
        slots_ref[h : h + 1, :] = slot
        data = jnp.concatenate(
            [q_ref[:, head_cols(h)], k_ref[:, head_cols(h)], v_ref[:, head_cols(h)], ones], axis=1
        )
        placed = dot_nn(slot_onehot(slot), data)
        used = placed[:, 3 * HD :]
        mark = jnp.where(first_lane, (1.0 - used) * EMPTY_MARK, 0.0)
        where = pl.ds(h, rows, stride=heads)
        wide[0, where, :] = placed[:, :HD]
        wide[1, where, :] = placed[:, HD : 2 * HD] + mark
        wide[2, where, :] = placed[:, 2 * HD : 3 * HD]
    for t in range(3):
        out_ref[:, t * HD : (t + 1) * HD] = wide[t].astype(jnp.bfloat16)


def collect_kernel(*refs):
    start = 0
    for ref in refs[:-1]:
        refs[-1][start : start + ref.shape[0], :] = ref[...]
        start += ref.shape[0]


def grad_kernel(slots_ref, *refs):
    grads, own_core, other_core = refs[:5], refs[5:9], refs[9:13]
    out_ref, wt_ref, wide = refs[13:]
    heads = slots_ref.shape[0]
    rows = CLUSTERS * CAP
    seq, y = lax.axis_index("seq"), lax.axis_index("head")
    z, x, core = seq // 8, lax.rem(seq // 2, 4), lax.rem(seq, 2)
    depth = own_core[0].shape[0] // 8
    for other, refs_of in enumerate((own_core, other_core)):
        side = core if other == 0 else 1 - core
        way = 1 - 2 * side
        for x_of, ref in zip((x, x - way, x + way, x + 2), refs_of):
            blocks = [(z, side), (z + 4, side)]
            for d in (1, 2, 3):
                blocks += [(z - d * way, side), (z - d * way, 1 - side)]
            for i, (z_of, core_of) in enumerate(blocks):
                row = lax.rem(z_of + 8, 8) * 8 + lax.rem(x_of + 4, 4) * 2 + core_of
                start = pl.multiple_of(row * depth, depth)
                wt_ref[pl.ds(start, depth), :] = ref[i * depth : (i + 1) * depth, :]
    total = None
    own, right, across_up, across_down, left = [ref[...] for ref in grads]
    across = jnp.concatenate([across_up, across_down], axis=0)
    for d, held in enumerate((own, right, across, left)):
        cols = held.shape[1]
        start = pl.multiple_of(lax.rem(y + (4 - d), 4) * cols, cols)
        part = dot_nn(held, wt_ref[pl.ds(start, cols), :])
        total = part if total is None else total + part
    grad = total.astype(jnp.bfloat16)
    for h in range(heads):
        placed = dot_nn(slot_onehot(slots_ref[h : h + 1, :]), grad[:, h * HD : (h + 1) * HD])
        wide[pl.ds(h, rows, stride=heads), :] = placed
    out_ref[...] = wide[...].astype(jnp.bfloat16)


def split_heads(x_ref, wide):
    for t in range(wide.shape[0]):
        wide[t] = x_ref[:, t * HD : (t + 1) * HD].astype(jnp.float32)


def scores_of(q, k, k_wide):
    first = lax.broadcasted_iota(jnp.int32, k.shape, 1) == 0
    mask = jnp.where(first & (k_wide > EMPTY_MARK / 2), -1e30, 0.0).astype(jnp.bfloat16)
    ones = jnp.ones(q.shape, jnp.bfloat16)
    return dot_nt(jnp.concatenate([k, mask], axis=1), jnp.concatenate([q, ones], axis=1))


def forward_kernel(x_ref, att_ref, heads_ref, probs_ref, att_wide_ref, wide, back):
    rows = CLUSTERS * CAP
    h = pl.program_id(0)

    @pl.when(h == 0)
    def _():
        split_heads(x_ref, wide)

    where = pl.ds(h, rows, stride=x_ref.shape[0] // rows)
    q = wide[0, where, :].astype(jnp.bfloat16)
    k_wide = wide[1, where, :]
    k = k_wide.astype(jnp.bfloat16)
    v = wide[2, where, :].astype(jnp.bfloat16)
    heads_ref[0] = q
    heads_ref[1] = k
    heads_ref[2] = v
    scores = scores_of(q, k, k_wide)
    top = jnp.max(scores, axis=0, keepdims=True)
    weights = jnp.exp2((scores - top) * (SCALE * LOG2E))
    probs = weights * (1.0 / jnp.sum(weights, axis=0, keepdims=True))
    probs_ref[0] = probs
    high = probs.astype(jnp.bfloat16)
    rest = probs - high.astype(jnp.float32)
    middle = rest.astype(jnp.bfloat16)
    low = (rest - middle.astype(jnp.float32)).astype(jnp.bfloat16)
    att = dot_tn(v, high)
    att_wide_ref[0] = att + (dot_tn(v, middle) + dot_tn(v, low))
    back[where, :] = att.T

    @pl.when(h == pl.num_programs(0) - 1)
    def _():
        att_ref[...] = back[...].astype(jnp.bfloat16)


def backward_kernel(g_ref, heads_ref, probs_ref, att_ref, out_ref, wide, back):
    rows = CLUSTERS * CAP
    h = pl.program_id(0)

    @pl.when(h == 0)
    def _():
        split_heads(g_ref, wide)

    where = pl.ds(h, rows, stride=g_ref.shape[0] // rows)
    g_wide = wide[0, where, :]
    g = g_wide.astype(jnp.bfloat16)
    q, k, v = heads_ref[0], heads_ref[1], heads_ref[2]
    probs = probs_ref[0]
    delta = jnp.sum(g_wide.T * att_ref[0], axis=0, keepdims=True)
    dscores = (probs * (dot_nt(v, g) - delta)).astype(jnp.bfloat16)
    back[0, where, :] = dot_tn(k, dscores).T * SCALE
    back[1, where, :] = dot_nn(dscores, q) * SCALE
    back[2, where, :] = dot_nn(probs.astype(jnp.bfloat16), g)

    @pl.when(h == pl.num_programs(0) - 1)
    def _():
        for t in range(3):
            out_ref[:, t * HD : (t + 1) * HD] = back[t].astype(jnp.bfloat16)


def mixed_kernel(slots_ref, att_ref, wt_ref, own_ref, s1, s2, s3, wide):
    heads = slots_ref.shape[0]
    rows = CLUSTERS * CAP
    y = lax.axis_index("head")
    wide[...] = att_ref[...].astype(jnp.float32)
    pieces = []
    for h in range(heads):
        held = wide[pl.ds(h, rows, stride=heads), :].astype(jnp.bfloat16)
        pieces.append(dot_nn(token_onehot(slots_ref[h : h + 1, :]), held).astype(jnp.bfloat16))
    att = jnp.concatenate(pieces, axis=1)
    for d, s_ref in enumerate((own_ref, s1, s2, s3)):
        cols = s_ref.shape[1]
        start = pl.multiple_of(lax.rem(y + d, 4) * cols, cols)
        s_ref[...] = dot_nt(att, wt_ref[pl.ds(start, cols), :]).astype(s_ref.dtype)


def unpack_kernel(slots_ref, x_ref, dq_ref, dk_ref, dv_ref, wide):
    heads = slots_ref.shape[0]
    rows = CLUSTERS * CAP
    for t in range(3):
        wide[t] = x_ref[:, t * HD : (t + 1) * HD].astype(jnp.float32)
    for h in range(heads):
        where = pl.ds(h, rows, stride=heads)
        held = jnp.concatenate(
            [wide[t, where, :].astype(jnp.bfloat16) for t in range(3)], axis=1
        )
        got = dot_nn(token_onehot(slots_ref[h : h + 1, :]), held).astype(jnp.bfloat16)
        for t, ref in enumerate((dq_ref, dk_ref, dv_ref)):
            ref[:, head_cols(h)] = got[:, t * HD : (t + 1) * HD]


def call(kernel, out, scratch, count):
    return pl.pallas_call(
        kernel,
        out_shape=out,
        in_specs=[VMEM] * count,
        out_specs=jax.tree.map(lambda _: VMEM, out),
        scratch_shapes=scratch,
        compiler_params=PARAMS,
    )


def far_out(shape):
    return pltpu.HBM(shape, jnp.bfloat16)


def sds(shape, dtype=jnp.bfloat16):
    return jax.ShapeDtypeStruct(shape, dtype)


def near(x):
    return pltpu.with_memory_space_constraint(x, pltpu.VMEM)


def exchange(x):
    return lax.all_to_all(x, "seq", split_axis=0, concat_axis=0, tiled=True)


def local(query, key, value, mixed_grad, out_weight, cluster):
    tokens = query.shape[0]
    heads = cluster.shape[0]
    rows = CLUSTERS * CAP
    slots_all = heads * rows

    def turn(x, d):
        return lax.ppermute(x, "head", [(i, (i + d) % 4) for i in range(4)])

    spots = [(z, x, c) for z in range(8) for x in range(4) for c in range(2)]

    def place(z, x, c):
        return z % 8 * 8 + x % 4 * 2 + c % 2

    def along(x, move):
        return lax.ppermute(x, "seq", [(place(*s), place(*move(*s))) for s in spots])

    shard = out_weight.T
    depth, width = shard.shape
    pair = jnp.concatenate([shard, along(shard, lambda z, x, c: (z, x, c + 1))], axis=0)
    far = along(shard, lambda z, x, c: (z + 4, x, c))
    near_by = [along(pair, lambda z, x, c, d=d: (z + d * (1 - 2 * c), x, c)) for d in (1, 2, 3)]
    column = call(collect_kernel, sds((8 * depth, width)), [], 5)(shard, far, *near_by)
    right, left = turn(mixed_grad, 1), turn(mixed_grad, 3)

    payload, slots = call(
        pack_kernel,
        (far_out((slots_all, 3 * HD)), sds((heads, tokens), jnp.int32)),
        [pltpu.VMEM((3, slots_all, HD), jnp.float32)],
        4,
    )(cluster.transpose(0, 2, 1), query, key, value)
    payload, column = lax.optimization_barrier((payload, column))
    arrived = exchange(payload)
    onward = lambda x: along(x, lambda z, x, c: (z, x + 1 - 2 * c, c))
    passed = onward(column)
    against = along(column, lambda z, x, c: (z, x - 1 + 2 * c, c))
    half = tokens // 2
    across = [turn(right[:half], 1), turn(left[half:], 3)]
    relayed = onward(passed)
    relayed, *across = lax.optimization_barrier((relayed, *across))
    own_core = [column, passed, against, relayed]
    other_core = [along(part, lambda z, x, c: (z, x, c + 1)) for part in own_core]


    by_head = lambda *shape: pl.BlockSpec(shape, lambda h: (h, 0, 0))
    att, held, probs, att_wide = pl.pallas_call(
        forward_kernel,
        grid=(heads,),
        out_shape=(
            far_out((slots_all, HD)),
            sds((heads * 3, rows, HD)),
            sds((heads, rows, rows), jnp.float32),
            sds((heads, HD, rows), jnp.float32),
        ),
        in_specs=[pl.BlockSpec((slots_all, 3 * HD), lambda h: (0, 0))],
        out_specs=(
            pl.BlockSpec((slots_all, HD), lambda h: (0, 0)),
            by_head(3, rows, HD),
            by_head(1, rows, rows),
            by_head(1, HD, rows),
        ),
        scratch_shapes=[
            pltpu.VMEM((3, slots_all, HD), jnp.float32),
            pltpu.VMEM((slots_all, HD), jnp.float32),
        ],
        compiler_params=PARAMS,
    )(near(arrived))

    grad_payload, wt = call(
        grad_kernel,
        (far_out((slots_all, HD)), sds((64 * depth, width))),
        [pltpu.VMEM((slots_all, HD), jnp.float32)],
        14,
    )(slots, mixed_grad, right, *across, left, *own_core, *other_core)
    grad_arrived = exchange(grad_payload)
    att, grad_arrived = lax.optimization_barrier((att, grad_arrived))
    att_back = exchange(att)

    done = pl.pallas_call(
        backward_kernel,
        grid=(heads,),
        out_shape=far_out((slots_all, 3 * HD)),
        in_specs=[
            pl.BlockSpec((slots_all, HD), lambda h: (0, 0)),
            by_head(3, rows, HD),
            by_head(1, rows, rows),
            by_head(1, HD, rows),
        ],
        out_specs=pl.BlockSpec((slots_all, 3 * HD), lambda h: (0, 0)),
        scratch_shapes=[
            pltpu.VMEM((1, slots_all, HD), jnp.float32),
            pltpu.VMEM((3, slots_all, HD), jnp.float32),
        ],
        compiler_params=PARAMS,
    )(near(grad_arrived), held, probs, att_wide)
    back = exchange(done)

    cols = mixed_grad.shape[1]
    own, *sends = call(
        mixed_kernel,
        (sds((tokens, cols), jnp.float32),) + (sds((tokens, cols)),) * 3,
        [pltpu.VMEM((slots_all, HD), jnp.float32)],
        3,
    )(slots, near(att_back), near(wt))
    mixed = own
    for d, part in zip((1, 2, 3), sends):
        mixed = mixed + turn(part, d).astype(jnp.float32)
    mixed = mixed.astype(jnp.bfloat16)

    query_grad, key_grad, value_grad = call(
        unpack_kernel,
        (sds((tokens, heads * HD)),) * 3,
        [pltpu.VMEM((3, slots_all, HD), jnp.float32)],
        2,
    )(slots, near(back))
    return (mixed, query_grad, key_grad, value_grad)


def solution(mesh):
    placed = (
        P("seq", "head"),
        P("seq", "head"),
        P("seq", "head"),
        P("seq", "head"),
        P("head", "seq"),
        P("head", "seq", None),
    )
    return jax.shard_map(
        local,
        mesh=mesh,
        in_specs=placed,
        out_specs=(P("seq", "head"), P("seq", "head"), P("seq", "head"), P("seq", "head")),
        check_vma=False,
    )
```

```python
import functools
import math

import jax
import jax.numpy as jnp
from jax import lax
from jax.experimental import pallas as pl
from jax.experimental.pallas import tpu as pltpu
from jax.sharding import PartitionSpec as P

HD = 128
CLUSTERS = 64
CAP = 12
EMPTY_MARK = 128.0
SCALE = 1.0 / math.sqrt(HD)
LOG2E = math.log2(math.e)

VMEM = pl.BlockSpec(memory_space=pltpu.VMEM)
PARAMS = pltpu.CompilerParams(vmem_limit_bytes=32 * 1024 * 1024)


def dot_nt(a, b):
    return lax.dot_general(a, b, (((1,), (1,)), ((), ())), preferred_element_type=jnp.float32)


def dot_tn(a, b):
    return lax.dot_general(a, b, (((0,), (0,)), ((), ())), preferred_element_type=jnp.float32)


def dot_nn(a, b):
    return jnp.dot(a, b, preferred_element_type=jnp.float32)


def head_cols(h):
    return pl.ds(h * HD, HD)


def slot_onehot(slot_row):
    tokens = slot_row.shape[1]
    place = lax.broadcasted_iota(jnp.int32, (CLUSTERS * CAP, tokens), 0)
    return jnp.where(place == slot_row, 1.0, 0.0).astype(jnp.bfloat16)


def token_onehot(slot_row):
    tokens = slot_row.shape[1]
    spread = jnp.broadcast_to(slot_row.astype(jnp.float32), (HD, tokens)).T
    lane = lax.broadcasted_iota(jnp.int32, (tokens, HD), 1).astype(jnp.float32)
    pieces = [
        jnp.where(spread == lane + float(start), 1.0, 0.0).astype(jnp.bfloat16)
        for start in range(0, CLUSTERS * CAP, HD)
    ]
    return jnp.concatenate(pieces, axis=1)


def pack_kernel(ids_ref, q_ref, k_ref, v_ref, out_ref, slots_ref, wide):
    heads, _, tokens = ids_ref.shape
    rows = CLUSTERS * CAP
    before = (
        lax.broadcasted_iota(jnp.int32, (tokens, tokens), 0)
        < lax.broadcasted_iota(jnp.int32, (tokens, tokens), 1)
    )
    before = jnp.where(before, 1.0, 0.0).astype(jnp.bfloat16)
    cluster = lax.broadcasted_iota(jnp.int32, (CLUSTERS, tokens), 0)
    ones = jnp.ones((tokens, HD), jnp.bfloat16)
    first_lane = lax.broadcasted_iota(jnp.int32, (rows, HD), 1) == 0
    for h in range(heads):
        ids = ids_ref[h]
        named = jnp.where(cluster == ids, 1.0, 0.0)
        earlier = dot_nn(named.astype(jnp.bfloat16), before)
        rank = jnp.sum(named * earlier, axis=0, keepdims=True)
        slot = ids * CAP + rank.astype(jnp.int32)
        slots_ref[h : h + 1, :] = slot
        data = jnp.concatenate(
            [q_ref[:, head_cols(h)], k_ref[:, head_cols(h)], v_ref[:, head_cols(h)], ones], axis=1
        )
        placed = dot_nn(slot_onehot(slot), data)
        used = placed[:, 3 * HD :]
        mark = jnp.where(first_lane, (1.0 - used) * EMPTY_MARK, 0.0)
        where = pl.ds(h, rows, stride=heads)
        wide[0, where, :] = placed[:, :HD]
        wide[1, where, :] = placed[:, HD : 2 * HD] + mark
        wide[2, where, :] = placed[:, 2 * HD : 3 * HD]
    for t in range(3):
        out_ref[:, t * HD : (t + 1) * HD] = wide[t].astype(jnp.bfloat16)


def collect_kernel(*refs):
    start = 0
    for ref in refs[:-1]:
        refs[-1][start : start + ref.shape[0], :] = ref[...]
        start += ref.shape[0]


def grad_kernel(slots_ref, *refs):
    grads, own_core, other_core = refs[:5], refs[5:9], refs[9:13]
    out_ref, wt_ref, wide = refs[13:]
    heads = slots_ref.shape[0]
    rows = CLUSTERS * CAP
    seq, y = lax.axis_index("seq"), lax.axis_index("head")
    z, x, core = seq // 8, lax.rem(seq // 2, 4), lax.rem(seq, 2)
    depth = own_core[0].shape[0] // 8
    for other, refs_of in enumerate((own_core, other_core)):
        side = core if other == 0 else 1 - core
        way = 1 - 2 * side
        for x_of, ref in zip((x, x - way, x + way, x + 2), refs_of):
            blocks = [(z, side), (z + 4, side)]
            for d in (1, 2, 3):
                blocks += [(z - d * way, side), (z - d * way, 1 - side)]
            for i, (z_of, core_of) in enumerate(blocks):
                row = lax.rem(z_of + 8, 8) * 8 + lax.rem(x_of + 4, 4) * 2 + core_of
                start = pl.multiple_of(row * depth, depth)
                wt_ref[pl.ds(start, depth), :] = ref[i * depth : (i + 1) * depth, :]
    total = None
    own, right, across_up, across_down, left = [ref[...] for ref in grads]
    across = jnp.concatenate([across_up, across_down], axis=0)
    for d, held in enumerate((own, right, across, left)):
        cols = held.shape[1]
        start = pl.multiple_of(lax.rem(y + (4 - d), 4) * cols, cols)
        part = dot_nn(held, wt_ref[pl.ds(start, cols), :])
        total = part if total is None else total + part
    grad = total.astype(jnp.bfloat16)
    for h in range(heads):
        placed = dot_nn(slot_onehot(slots_ref[h : h + 1, :]), grad[:, h * HD : (h + 1) * HD])
        wide[pl.ds(h, rows, stride=heads), :] = placed
    out_ref[...] = wide[...].astype(jnp.bfloat16)


def split_heads(x_ref, wide):
    for t in range(wide.shape[0]):
        wide[t] = x_ref[:, t * HD : (t + 1) * HD].astype(jnp.float32)


def scores_of(q, k, k_wide):
    first = lax.broadcasted_iota(jnp.int32, k.shape, 1) == 0
    mask = jnp.where(first & (k_wide > EMPTY_MARK / 2), -1e30, 0.0).astype(jnp.bfloat16)
    ones = jnp.ones(q.shape, jnp.bfloat16)
    return dot_nt(jnp.concatenate([k, mask], axis=1), jnp.concatenate([q, ones], axis=1))


def forward_kernel(x_ref, att_ref, heads_ref, probs_ref, att_wide_ref, wide, back):
    rows = CLUSTERS * CAP
    h = pl.program_id(0)

    @pl.when(h == 0)
    def _():
        split_heads(x_ref, wide)

    where = pl.ds(h, rows, stride=x_ref.shape[0] // rows)
    q = wide[0, where, :].astype(jnp.bfloat16)
    k_wide = wide[1, where, :]
    k = k_wide.astype(jnp.bfloat16)
    v = wide[2, where, :].astype(jnp.bfloat16)
    heads_ref[0] = q
    heads_ref[1] = k
    heads_ref[2] = v
    scores = scores_of(q, k, k_wide)
    top = jnp.max(scores, axis=0, keepdims=True)
    weights = jnp.exp2((scores - top) * (SCALE * LOG2E))
    probs = weights * (1.0 / jnp.sum(weights, axis=0, keepdims=True))
    probs_ref[0] = probs
    high = probs.astype(jnp.bfloat16)
    rest = probs - high.astype(jnp.float32)
    middle = rest.astype(jnp.bfloat16)
    low = (rest - middle.astype(jnp.float32)).astype(jnp.bfloat16)
    att = dot_tn(v, high)
    att_wide_ref[0] = att + (dot_tn(v, middle) + dot_tn(v, low))
    back[where, :] = att.T

    @pl.when(h == pl.num_programs(0) - 1)
    def _():
        att_ref[...] = back[...].astype(jnp.bfloat16)


def backward_kernel(g_ref, heads_ref, probs_ref, att_ref, out_ref, wide, back):
    rows = CLUSTERS * CAP
    h = pl.program_id(0)

    @pl.when(h == 0)
    def _():
        split_heads(g_ref, wide)

    where = pl.ds(h, rows, stride=g_ref.shape[0] // rows)
    g_wide = wide[0, where, :]
    g = g_wide.astype(jnp.bfloat16)
    q, k, v = heads_ref[0], heads_ref[1], heads_ref[2]
    probs = probs_ref[0]
    delta = jnp.sum(g_wide.T * att_ref[0], axis=0, keepdims=True)
    dscores = (probs * (dot_nt(v, g) - delta)).astype(jnp.bfloat16)
    back[0, where, :] = dot_tn(k, dscores).T * SCALE
    back[1, where, :] = dot_nn(dscores, q) * SCALE
    back[2, where, :] = dot_nn(probs.astype(jnp.bfloat16), g)

    @pl.when(h == pl.num_programs(0) - 1)
    def _():
        for t in range(3):
            out_ref[:, t * HD : (t + 1) * HD] = back[t].astype(jnp.bfloat16)


def mixed_kernel(slots_ref, att_ref, wt_ref, own_ref, s1, s2, s3, wide):
    heads = slots_ref.shape[0]
    rows = CLUSTERS * CAP
    y = lax.axis_index("head")
    wide[...] = att_ref[...].astype(jnp.float32)
    pieces = []
    for h in range(heads):
        held = wide[pl.ds(h, rows, stride=heads), :].astype(jnp.bfloat16)
        pieces.append(dot_nn(token_onehot(slots_ref[h : h + 1, :]), held).astype(jnp.bfloat16))
    att = jnp.concatenate(pieces, axis=1)
    for d, s_ref in enumerate((own_ref, s1, s2, s3)):
        cols = s_ref.shape[1]
        start = pl.multiple_of(lax.rem(y + d, 4) * cols, cols)
        s_ref[...] = dot_nt(att, wt_ref[pl.ds(start, cols), :]).astype(s_ref.dtype)


def unpack_kernel(slots_ref, x_ref, dq_ref, dk_ref, dv_ref, wide):
    heads = slots_ref.shape[0]
    rows = CLUSTERS * CAP
    for t in range(3):
        wide[t] = x_ref[:, t * HD : (t + 1) * HD].astype(jnp.float32)
    for h in range(heads):
        where = pl.ds(h, rows, stride=heads)
        held = jnp.concatenate(
            [wide[t, where, :].astype(jnp.bfloat16) for t in range(3)], axis=1
        )
        got = dot_nn(token_onehot(slots_ref[h : h + 1, :]), held).astype(jnp.bfloat16)
        for t, ref in enumerate((dq_ref, dk_ref, dv_ref)):
            ref[:, head_cols(h)] = got[:, t * HD : (t + 1) * HD]


def call(kernel, out, scratch, count, micros=None):
    cost = None
    if micros is not None:
        cost = pl.CostEstimate(flops=int(micros * 1.15e9), bytes_accessed=0, transcendentals=0)
    return pl.pallas_call(
        kernel,
        cost_estimate=cost,
        out_shape=out,
        in_specs=[VMEM] * count,
        out_specs=jax.tree.map(lambda _: VMEM, out),
        scratch_shapes=scratch,
        compiler_params=PARAMS,
    )


def far_out(shape):
    return pltpu.HBM(shape, jnp.bfloat16)


def sds(shape, dtype=jnp.bfloat16):
    return jax.ShapeDtypeStruct(shape, dtype)


def near(x):
    return pltpu.with_memory_space_constraint(x, pltpu.VMEM)


def far(x):
    return pltpu.with_memory_space_constraint(x, pltpu.HBM)


def exchange(x):
    return lax.all_to_all(x, "seq", split_axis=0, concat_axis=0, tiled=True)


def local(query, key, value, mixed_grad, out_weight, cluster):
    tokens = query.shape[0]
    heads = cluster.shape[0]
    rows = CLUSTERS * CAP
    slots_all = heads * rows

    def turn(x, d):
        return lax.ppermute(x, "head", [(i, (i + d) % 4) for i in range(4)])

    spots = [(z, x, c) for z in range(8) for x in range(4) for c in range(2)]

    def place(z, x, c):
        return z % 8 * 8 + x % 4 * 2 + c % 2

    def along(x, move):
        return lax.ppermute(x, "seq", [(place(*s), place(*move(*s))) for s in spots])

    shard = out_weight.T
    depth, width = shard.shape
    pair = jnp.concatenate([shard, along(shard, lambda z, x, c: (z, x, c + 1))], axis=0)
    opposite = along(shard, lambda z, x, c: (z + 4, x, c))
    near_by = [along(pair, lambda z, x, c, d=d: (z + d * (1 - 2 * c), x, c)) for d in (1, 2, 3)]
    column = call(collect_kernel, sds((8 * depth, width)), [], 5, micros=60)(shard, opposite, *near_by)
    right, left = turn(mixed_grad, 1), turn(mixed_grad, 3)

    payload, slots = call(
        pack_kernel,
        (far_out((slots_all, 3 * HD)), sds((heads, tokens), jnp.int32)),
        [pltpu.VMEM((3, slots_all, HD), jnp.float32)],
        4,
    )(far(cluster.transpose(0, 2, 1)), far(query), far(key), far(value))
    arrived = exchange(payload)
    onward = lambda x: along(x, lambda z, x, c: (z, x + 1 - 2 * c, c))
    passed = onward(column)
    against = along(column, lambda z, x, c: (z, x - 1 + 2 * c, c))
    half = tokens // 2
    across = [turn(right[:half], 1), turn(left[half:], 3)]
    relayed = onward(passed)
    relayed, *across = lax.optimization_barrier((relayed, *across))
    own_core = [column, passed, against, relayed]
    other_core = [along(part, lambda z, x, c: (z, x, c + 1)) for part in own_core]


    by_head = lambda *shape: pl.BlockSpec(shape, lambda h: (h, 0, 0))
    att, held, probs, att_wide = pl.pallas_call(
        forward_kernel,
        grid=(heads,),
        out_shape=(
            far_out((slots_all, HD)),
            sds((heads * 3, rows, HD)),
            sds((heads, rows, rows), jnp.float32),
            sds((heads, HD, rows), jnp.float32),
        ),
        in_specs=[pl.BlockSpec((slots_all, 3 * HD), lambda h: (0, 0))],
        out_specs=(
            pl.BlockSpec((slots_all, HD), lambda h: (0, 0)),
            by_head(3, rows, HD),
            by_head(1, rows, rows),
            by_head(1, HD, rows),
        ),
        scratch_shapes=[
            pltpu.VMEM((3, slots_all, HD), jnp.float32),
            pltpu.VMEM((slots_all, HD), jnp.float32),
        ],
        compiler_params=PARAMS,
    )(near(arrived))

    grad_payload, wt = call(
        grad_kernel,
        (far_out((slots_all, HD)), sds((64 * depth, width))),
        [pltpu.VMEM((slots_all, HD), jnp.float32)],
        14,
    )(slots, mixed_grad, right, *across, left, *own_core, *other_core)
    grad_arrived = exchange(grad_payload)
    att, grad_arrived = lax.optimization_barrier((att, grad_arrived))
    att_back = exchange(att)

    done = pl.pallas_call(
        backward_kernel,
        grid=(heads,),
        out_shape=far_out((slots_all, 3 * HD)),
        in_specs=[
            pl.BlockSpec((slots_all, HD), lambda h: (0, 0)),
            by_head(3, rows, HD),
            by_head(1, rows, rows),
            by_head(1, HD, rows),
        ],
        out_specs=pl.BlockSpec((slots_all, 3 * HD), lambda h: (0, 0)),
        scratch_shapes=[
            pltpu.VMEM((1, slots_all, HD), jnp.float32),
            pltpu.VMEM((3, slots_all, HD), jnp.float32),
        ],
        compiler_params=PARAMS,
    )(near(grad_arrived), held, probs, att_wide)
    back = exchange(done)

    cols = mixed_grad.shape[1]
    own, *sends = call(
        mixed_kernel,
        (sds((tokens, cols), jnp.float32),) + (sds((tokens, cols)),) * 3,
        [pltpu.VMEM((slots_all, HD), jnp.float32)],
        3,
    )(slots, near(att_back), near(wt))
    mixed = own
    for d, part in zip((1, 2, 3), sends):
        mixed = mixed + turn(part, d).astype(jnp.float32)
    mixed = mixed.astype(jnp.bfloat16)

    query_grad, key_grad, value_grad = call(
        unpack_kernel,
        (sds((tokens, heads * HD)),) * 3,
        [pltpu.VMEM((3, slots_all, HD), jnp.float32)],
        2,
    )(slots, near(back))
    return (mixed, query_grad, key_grad, value_grad)


def solution(mesh):
    placed = (
        P("seq", "head"),
        P("seq", "head"),
        P("seq", "head"),
        P("seq", "head"),
        P("head", "seq"),
        P("head", "seq", None),
    )
    return jax.shard_map(
        local,
        mesh=mesh,
        in_specs=placed,
        out_specs=(P("seq", "head"), P("seq", "head"), P("seq", "head"), P("seq", "head")),
        check_vma=False,
    )
```

```python
import functools
import math

import jax
import jax.numpy as jnp
from jax import lax
from jax.experimental import pallas as pl
from jax.experimental.pallas import tpu as pltpu
from jax.sharding import PartitionSpec as P

HD = 128
CLUSTERS = 64
CAP = 12
EMPTY_MARK = 128.0
SCALE = 1.0 / math.sqrt(HD)
LOG2E = math.log2(math.e)

VMEM = pl.BlockSpec(memory_space=pltpu.VMEM)
PARAMS = pltpu.CompilerParams(vmem_limit_bytes=32 * 1024 * 1024)


def dot_nt(a, b):
    return lax.dot_general(a, b, (((1,), (1,)), ((), ())), preferred_element_type=jnp.float32)


def dot_tn(a, b):
    return lax.dot_general(a, b, (((0,), (0,)), ((), ())), preferred_element_type=jnp.float32)


def dot_nn(a, b):
    return jnp.dot(a, b, preferred_element_type=jnp.float32)


def head_cols(h):
    return pl.ds(h * HD, HD)


def slot_onehot(slot_row):
    tokens = slot_row.shape[1]
    place = lax.broadcasted_iota(jnp.int32, (CLUSTERS * CAP, tokens), 0)
    return jnp.where(place == slot_row, 1.0, 0.0).astype(jnp.bfloat16)


def token_onehot(slot_row):
    tokens = slot_row.shape[1]
    spread = jnp.broadcast_to(slot_row.astype(jnp.float32), (HD, tokens)).T
    lane = lax.broadcasted_iota(jnp.int32, (tokens, HD), 1).astype(jnp.float32)
    pieces = [
        jnp.where(spread == lane + float(start), 1.0, 0.0).astype(jnp.bfloat16)
        for start in range(0, CLUSTERS * CAP, HD)
    ]
    return jnp.concatenate(pieces, axis=1)


def pack_kernel(ids_ref, q_hbm, k_hbm, v_hbm, out_ref, slots_ref, wide, held, staged, arrive, leave):
    fetches = [
        pltpu.make_async_copy(hbm, held.at[t], arrive.at[t])
        for t, hbm in enumerate((q_hbm, k_hbm, v_hbm))
    ]
    for fetch in fetches:
        fetch.start()
    heads, _, tokens = ids_ref.shape
    rows = CLUSTERS * CAP
    before = (
        lax.broadcasted_iota(jnp.int32, (tokens, tokens), 0)
        < lax.broadcasted_iota(jnp.int32, (tokens, tokens), 1)
    )
    before = jnp.where(before, 1.0, 0.0).astype(jnp.bfloat16)
    cluster = lax.broadcasted_iota(jnp.int32, (CLUSTERS, tokens), 0)
    ones = jnp.ones((tokens, HD), jnp.bfloat16)
    first_lane = lax.broadcasted_iota(jnp.int32, (rows, HD), 1) == 0
    for h in range(heads):
        ids = ids_ref[h]
        named = jnp.where(cluster == ids, 1.0, 0.0)
        earlier = dot_nn(named.astype(jnp.bfloat16), before)
        rank = jnp.sum(named * earlier, axis=0, keepdims=True)
        slot = ids * CAP + rank.astype(jnp.int32)
        slots_ref[h : h + 1, :] = slot
    for fetch in fetches:
        fetch.wait()
    for h in range(heads):
        slot = slots_ref[h : h + 1, :]
        data = jnp.concatenate(
            [held[t, :, h * HD : (h + 1) * HD] for t in range(3)] + [ones], axis=1
        )
        placed = dot_nn(slot_onehot(slot), data)
        used = placed[:, 3 * HD :]
        mark = jnp.where(first_lane, (1.0 - used) * EMPTY_MARK, 0.0)
        where = pl.ds(h, rows, stride=heads)
        wide[0, where, :] = placed[:, :HD]
        wide[1, where, :] = placed[:, HD : 2 * HD] + mark
        wide[2, where, :] = placed[:, 2 * HD : 3 * HD]
    parts = staged.shape[0]
    span = staged.shape[1]
    sends = []
    for p in range(parts):
        some = slice(p * span, (p + 1) * span)
        for t in range(3):
            staged[p, :, t * HD : (t + 1) * HD] = wide[t, some, :].astype(jnp.bfloat16)
        send = pltpu.make_async_copy(staged.at[p], out_ref.at[some], leave.at[p])
        send.start()
        sends.append(send)
    for send in sends:
        send.wait()


def collect_kernel(*refs):
    start = 0
    for ref in refs[:-1]:
        refs[-1][start : start + ref.shape[0], :] = ref[...]
        start += ref.shape[0]


def grad_kernel(slots_ref, *refs):
    grads, own_core, other_core = refs[:5], refs[5:9], refs[9:13]
    out_ref, wt_ref, wide = refs[13:]
    heads = slots_ref.shape[0]
    rows = CLUSTERS * CAP
    seq, y = lax.axis_index("seq"), lax.axis_index("head")
    z, x, core = seq // 8, lax.rem(seq // 2, 4), lax.rem(seq, 2)
    depth = own_core[0].shape[0] // 8
    for other, refs_of in enumerate((own_core, other_core)):
        side = core if other == 0 else 1 - core
        way = 1 - 2 * side
        for x_of, ref in zip((x, x - way, x + way, x + 2), refs_of):
            blocks = [(z, side), (z + 4, side)]
            for d in (1, 2, 3):
                blocks += [(z - d * way, side), (z - d * way, 1 - side)]
            for i, (z_of, core_of) in enumerate(blocks):
                row = lax.rem(z_of + 8, 8) * 8 + lax.rem(x_of + 4, 4) * 2 + core_of
                start = pl.multiple_of(row * depth, depth)
                wt_ref[pl.ds(start, depth), :] = ref[i * depth : (i + 1) * depth, :]
    total = None
    own, right, across_up, across_down, left = [ref[...] for ref in grads]
    across = jnp.concatenate([across_up, across_down], axis=0)
    for d, held in enumerate((own, right, across, left)):
        cols = held.shape[1]
        start = pl.multiple_of(lax.rem(y + (4 - d), 4) * cols, cols)
        part = dot_nn(held, wt_ref[pl.ds(start, cols), :])
        total = part if total is None else total + part
    grad = total.astype(jnp.bfloat16)
    for h in range(heads):
        placed = dot_nn(slot_onehot(slots_ref[h : h + 1, :]), grad[:, h * HD : (h + 1) * HD])
        wide[pl.ds(h, rows, stride=heads), :] = placed
    out_ref[...] = wide[...].astype(jnp.bfloat16)


def split_heads(x_ref, wide):
    for t in range(wide.shape[0]):
        wide[t] = x_ref[:, t * HD : (t + 1) * HD].astype(jnp.float32)


def scores_of(q, k, k_wide):
    first = lax.broadcasted_iota(jnp.int32, k.shape, 1) == 0
    mask = jnp.where(first & (k_wide > EMPTY_MARK / 2), -1e30, 0.0).astype(jnp.bfloat16)
    ones = jnp.ones(q.shape, jnp.bfloat16)
    return dot_nt(jnp.concatenate([k, mask], axis=1), jnp.concatenate([q, ones], axis=1))


def forward_kernel(x_ref, att_ref, heads_ref, probs_ref, att_wide_ref, wide, back):
    rows = CLUSTERS * CAP
    h = pl.program_id(0)

    @pl.when(h == 0)
    def _():
        split_heads(x_ref, wide)

    where = pl.ds(h, rows, stride=x_ref.shape[0] // rows)
    q = wide[0, where, :].astype(jnp.bfloat16)
    k_wide = wide[1, where, :]
    k = k_wide.astype(jnp.bfloat16)
    v = wide[2, where, :].astype(jnp.bfloat16)
    heads_ref[0] = q
    heads_ref[1] = k
    heads_ref[2] = v
    scores = scores_of(q, k, k_wide)
    top = jnp.max(scores, axis=0, keepdims=True)
    weights = jnp.exp2((scores - top) * (SCALE * LOG2E))
    probs = weights * (1.0 / jnp.sum(weights, axis=0, keepdims=True))
    probs_ref[0] = probs
    high = probs.astype(jnp.bfloat16)
    rest = probs - high.astype(jnp.float32)
    middle = rest.astype(jnp.bfloat16)
    low = (rest - middle.astype(jnp.float32)).astype(jnp.bfloat16)
    att = dot_tn(v, high)
    att_wide_ref[0] = att + (dot_tn(v, middle) + dot_tn(v, low))
    back[where, :] = att.T

    @pl.when(h == pl.num_programs(0) - 1)
    def _():
        att_ref[...] = back[...].astype(jnp.bfloat16)


def backward_kernel(g_ref, heads_ref, probs_ref, att_ref, out_ref, wide, back):
    rows = CLUSTERS * CAP
    h = pl.program_id(0)

    @pl.when(h == 0)
    def _():
        split_heads(g_ref, wide)

    where = pl.ds(h, rows, stride=g_ref.shape[0] // rows)
    g_wide = wide[0, where, :]
    g = g_wide.astype(jnp.bfloat16)
    q, k, v = heads_ref[0], heads_ref[1], heads_ref[2]
    probs = probs_ref[0]
    delta = jnp.sum(g_wide.T * att_ref[0], axis=0, keepdims=True)
    dscores = (probs * (dot_nt(v, g) - delta)).astype(jnp.bfloat16)
    back[0, where, :] = dot_tn(k, dscores).T * SCALE
    back[1, where, :] = dot_nn(dscores, q) * SCALE
    back[2, where, :] = dot_nn(probs.astype(jnp.bfloat16), g)

    @pl.when(h == pl.num_programs(0) - 1)
    def _():
        for t in range(3):
            out_ref[:, t * HD : (t + 1) * HD] = back[t].astype(jnp.bfloat16)


def mixed_kernel(slots_ref, att_ref, wt_ref, own_ref, s1, s2, s3, wide):
    heads = slots_ref.shape[0]
    rows = CLUSTERS * CAP
    y = lax.axis_index("head")
    wide[...] = att_ref[...].astype(jnp.float32)
    pieces = []
    for h in range(heads):
        held = wide[pl.ds(h, rows, stride=heads), :].astype(jnp.bfloat16)
        pieces.append(dot_nn(token_onehot(slots_ref[h : h + 1, :]), held).astype(jnp.bfloat16))
    att = jnp.concatenate(pieces, axis=1)
    for d, s_ref in enumerate((own_ref, s1, s2, s3)):
        cols = s_ref.shape[1]
        start = pl.multiple_of(lax.rem(y + d, 4) * cols, cols)
        s_ref[...] = dot_nt(att, wt_ref[pl.ds(start, cols), :]).astype(s_ref.dtype)


def unpack_kernel(slots_ref, x_ref, dq_ref, dk_ref, dv_ref, wide):
    heads = slots_ref.shape[0]
    rows = CLUSTERS * CAP
    for t in range(3):
        wide[t] = x_ref[:, t * HD : (t + 1) * HD].astype(jnp.float32)
    for h in range(heads):
        where = pl.ds(h, rows, stride=heads)
        held = jnp.concatenate(
            [wide[t, where, :].astype(jnp.bfloat16) for t in range(3)], axis=1
        )
        got = dot_nn(token_onehot(slots_ref[h : h + 1, :]), held).astype(jnp.bfloat16)
        for t, ref in enumerate((dq_ref, dk_ref, dv_ref)):
            ref[:, head_cols(h)] = got[:, t * HD : (t + 1) * HD]


def call(kernel, out, scratch, count, micros=None):
    cost = None
    if micros is not None:
        cost = pl.CostEstimate(flops=int(micros * 1.15e9), bytes_accessed=0, transcendentals=0)
    return pl.pallas_call(
        kernel,
        cost_estimate=cost,
        out_shape=out,
        in_specs=[VMEM] * count,
        out_specs=jax.tree.map(lambda _: VMEM, out),
        scratch_shapes=scratch,
        compiler_params=PARAMS,
    )


def far_out(shape):
    return pltpu.HBM(shape, jnp.bfloat16)


def sds(shape, dtype=jnp.bfloat16):
    return jax.ShapeDtypeStruct(shape, dtype)


def near(x):
    return pltpu.with_memory_space_constraint(x, pltpu.VMEM)


def far(x):
    return pltpu.with_memory_space_constraint(x, pltpu.HBM)


def exchange(x):
    return lax.all_to_all(x, "seq", split_axis=0, concat_axis=0, tiled=True)


def local(query, key, value, mixed_grad, out_weight, cluster):
    tokens = query.shape[0]
    heads = cluster.shape[0]
    rows = CLUSTERS * CAP
    slots_all = heads * rows

    def turn(x, d):
        return lax.ppermute(x, "head", [(i, (i + d) % 4) for i in range(4)])

    spots = [(z, x, c) for z in range(8) for x in range(4) for c in range(2)]

    def place(z, x, c):
        return z % 8 * 8 + x % 4 * 2 + c % 2

    def along(x, move):
        return lax.ppermute(x, "seq", [(place(*s), place(*move(*s))) for s in spots])

    shard = out_weight.T
    depth, width = shard.shape
    partner = along(shard, lambda z, x, c: (z, x, c + 1))
    pair = call(collect_kernel, sds((2 * depth, width)), [], 2)(shard, partner)
    opposite = along(shard, lambda z, x, c: (z + 4, x, c))
    near_by = [along(pair, lambda z, x, c, d=d: (z + d * (1 - 2 * c), x, c)) for d in (1, 2, 3)]
    column = call(collect_kernel, sds((8 * depth, width)), [], 5, micros=60)(shard, opposite, *near_by)
    right, left = turn(mixed_grad, 1), turn(mixed_grad, 3)

    hbm = pl.BlockSpec(memory_space=pl.ANY)
    payload, slots = pl.pallas_call(
        pack_kernel,
        out_shape=(far_out((slots_all, 3 * HD)), sds((heads, tokens), jnp.int32)),
        in_specs=[VMEM, hbm, hbm, hbm],
        out_specs=(hbm, VMEM),
        scratch_shapes=[
            pltpu.VMEM((3, slots_all, HD), jnp.float32),
            pltpu.VMEM((3, tokens, heads * HD), jnp.bfloat16),
            pltpu.VMEM((4, slots_all // 4, 3 * HD), jnp.bfloat16),
            pltpu.SemaphoreType.DMA((3,)),
            pltpu.SemaphoreType.DMA((4,)),
        ],
        compiler_params=PARAMS,
    )(far(cluster.transpose(0, 2, 1)), far(query), far(key), far(value))
    arrived = exchange(payload)
    onward = lambda x: along(x, lambda z, x, c: (z, x + 1 - 2 * c, c))
    passed = onward(column)
    against = along(column, lambda z, x, c: (z, x - 1 + 2 * c, c))
    half = tokens // 2
    across = [turn(right[:half], 1), turn(left[half:], 3)]
    relayed = onward(passed)
    relayed, *across = lax.optimization_barrier((relayed, *across))
    own_core = [column, passed, against, relayed]
    other_core = [along(part, lambda z, x, c: (z, x, c + 1)) for part in own_core]


    by_head = lambda *shape: pl.BlockSpec(shape, lambda h: (h, 0, 0))
    att, held, probs, att_wide = pl.pallas_call(
        forward_kernel,
        grid=(heads,),
        out_shape=(
            far_out((slots_all, HD)),
            sds((heads * 3, rows, HD)),
            sds((heads, rows, rows), jnp.float32),
            sds((heads, HD, rows), jnp.float32),
        ),
        in_specs=[pl.BlockSpec((slots_all, 3 * HD), lambda h: (0, 0))],
        out_specs=(
            pl.BlockSpec((slots_all, HD), lambda h: (0, 0)),
            by_head(3, rows, HD),
            by_head(1, rows, rows),
            by_head(1, HD, rows),
        ),
        scratch_shapes=[
            pltpu.VMEM((3, slots_all, HD), jnp.float32),
            pltpu.VMEM((slots_all, HD), jnp.float32),
        ],
        compiler_params=PARAMS,
    )(near(arrived))

    grad_payload, wt = call(
        grad_kernel,
        (far_out((slots_all, HD)), sds((64 * depth, width))),
        [pltpu.VMEM((slots_all, HD), jnp.float32)],
        14,
    )(slots, mixed_grad, right, *across, left, *own_core, *other_core)
    grad_arrived = exchange(grad_payload)
    att, grad_arrived = lax.optimization_barrier((att, grad_arrived))
    att_back = exchange(att)

    done = pl.pallas_call(
        backward_kernel,
        grid=(heads,),
        out_shape=far_out((slots_all, 3 * HD)),
        in_specs=[
            pl.BlockSpec((slots_all, HD), lambda h: (0, 0)),
            by_head(3, rows, HD),
            by_head(1, rows, rows),
            by_head(1, HD, rows),
        ],
        out_specs=pl.BlockSpec((slots_all, 3 * HD), lambda h: (0, 0)),
        scratch_shapes=[
            pltpu.VMEM((1, slots_all, HD), jnp.float32),
            pltpu.VMEM((3, slots_all, HD), jnp.float32),
        ],
        compiler_params=PARAMS,
    )(near(grad_arrived), held, probs, att_wide)
    back = exchange(done)

    cols = mixed_grad.shape[1]
    own, *sends = call(
        mixed_kernel,
        (sds((tokens, cols), jnp.float32),) + (sds((tokens, cols)),) * 3,
        [pltpu.VMEM((slots_all, HD), jnp.float32)],
        3,
    )(slots, far(att_back), near(wt))
    mixed = own
    for d, part in zip((1, 2, 3), sends):
        mixed = mixed + turn(part, d).astype(jnp.float32)
    mixed = mixed.astype(jnp.bfloat16)

    query_grad, key_grad, value_grad = call(
        unpack_kernel,
        (sds((tokens, heads * HD)),) * 3,
        [pltpu.VMEM((3, slots_all, HD), jnp.float32)],
        2,
    )(slots, near(back))
    return (mixed, query_grad, key_grad, value_grad)


def solution(mesh):
    placed = (
        P("seq", "head"),
        P("seq", "head"),
        P("seq", "head"),
        P("seq", "head"),
        P("head", "seq"),
        P("head", "seq", None),
    )
    return jax.shard_map(
        local,
        mesh=mesh,
        in_specs=placed,
        out_specs=(P("seq", "head"), P("seq", "head"), P("seq", "head"), P("seq", "head")),
        check_vma=False,
    )
```
